32 devices in a mesh: expert: 16 (over z, y, core), attn: 2 (over x).
Axes of the slice: x: 2, y: 2, z: 4, core: 2. Of those that a mesh axis runs over, the one named last changes fastest.
Arguments:
- queries: bfloat16 [512, 64, 576], P('expert', 'attn'), may hold values from -6 to 6
- prompt_cache: bfloat16 [64, 256, 576], P('expert'), may hold values from -6 to 6
- beam_cache: bfloat16 [512, 16, 576], P('expert'), may hold values from -6 to 6
- new_latent: bfloat16 [512, 576], P('expert'), may hold values from -6 to 6
- parents: int32 [512], P('expert'), may hold values from 0 to 7
- lengths: int32 [64], P('expert'), may hold values from 32 to 256, as said below
- up_values: bfloat16 [64, 512, 128], P('attn'), may hold values from -0.25 to 0.25
- moe_input: bfloat16 [512, 7168], P('expert', 'attn'), may hold values from -6 to 6
- routes: int32 [512, 8], P('expert'), may hold values from 0 to 15, all different within a row; in each aligned block of 32 rows (0 to 31, 32 to 63, ...) at most 32 rows name the same one
- route_scores: float32 [512, 8], P('expert'), may hold values from 0.05 to 1
- w_gate: bfloat16 [16, 7168, 2048], P('expert', None, 'attn'), may hold values from -0.0625 to 0.0625
- w_up: bfloat16 [16, 7168, 2048], P('expert', None, 'attn'), may hold values from -0.0625 to 0.0625
- w_down: bfloat16 [16, 2048, 7168], P('expert', 'attn'), may hold values from -0.125 to 0.125
Outputs:
- attn_values: bfloat16 [512, 8192], P('expert', 'attn')
- moe_out: bfloat16 [512, 7168], P('expert', 'attn')
The draws below stay inside these ranges and needn't reach their ends.
Inputs may be any that keep to these rules, and one draw needn't show every extreme that they name: `lengths`: the longest prompt has exactly 256 valid positions. `routes`: each row names 8 different experts. Among the rows of one index of expert no expert is named by more than 32 rows, and in every draw some expert is named by exactly 32 of them.
All inputs are finite; a program needn't handle non-finite values.
Results may differ from the reference program's by a relative error of at most 0.012.
Values may be sent and summed in bfloat16 or wider, within the bound.
A program may use at most 128 MiB of HBM per device.

```python
import math
import jax
import jax.numpy as jnp
import numpy as np
from jax import lax

D = 7168
FF = 2048
HEADS = 64
LAT = 512
ROPE = 64
VHEAD = 128
TOPK = 8
BEAMS = 8
GEN = 16
CTX = 256
EXPERTS = 16
PROMPTS = 64
ROWS_DEV = 32
ROWS = 512
CAP = 32
N_EXPERT = 16
N_ATTN = 2


align_scale = 192.0 ** (-0.5)


query_peak = 6.0


def aligned_plan(key):
    parts_of = jax.random.split(key, 6)
    signs = jnp.where(jax.random.bernoulli(parts_of[0], 0.5, (PROMPTS, LAT + ROPE)), 1.0, -1.0).astype(jnp.float32)
    strength = jnp.exp(jax.random.uniform(parts_of[1], (PROMPTS,), jnp.float32, math.log(0.75), math.log(2.5)))
    beam_pick = jax.random.randint(parts_of[2], (PROMPTS,), 0, BEAMS)
    head_pick = jax.random.randint(parts_of[3], (PROMPTS,), 0, HEADS)
    span = CTX // 8
    first_pos = jax.random.randint(parts_of[4], (PROMPTS,), 0, span)
    second_pos = (first_pos + jax.random.randint(parts_of[5], (PROMPTS,), 1, span)) % span
    return (signs, strength, beam_pick, head_pick, first_pos, second_pos)


def column_sets():
    columns = jnp.arange(LAT + ROPE)
    in_set = (columns < LAT - LAT // 4) | (columns >= LAT)
    rope_part = columns >= LAT
    return (in_set, rope_part)


def draw_queries(key, part):
    plan = aligned_plan(key)
    signs = plan[0]
    beam_pick = plan[2]
    head_pick = plan[3]
    key = jax.random.fold_in(key, 11)
    base = jax.random.truncated_normal(key, -6.0, 6.0, (PROMPTS, BEAMS, HEADS, LAT + ROPE), jnp.float32)
    in_set, rope_part = column_sets()
    aligned = jnp.where(in_set[None, :], query_peak * signs, 0.0)
    chosen = (jnp.arange(BEAMS)[None, :, None] == beam_pick[:, None, None]) & (jnp.arange(HEADS)[None, None, :] == head_pick[:, None, None])
    result = jnp.where(chosen[..., None], aligned[:, None, None, :], base)
    return result.reshape(ROWS, HEADS, LAT + ROPE).astype(jnp.bfloat16)


def draw_prompt_cache(key, part):
    signs, strength, beam_pick, head_pick, first_pos, second_pos = aligned_plan(key)
    key = jax.random.fold_in(key, 13)
    base = jax.random.truncated_normal(key, -6.0, 6.0, (PROMPTS, CTX, LAT + ROPE), jnp.float32)
    in_set, rope_part = column_sets()
    first_key = strength[:, None] * signs
    lowered = 2.0 / (align_scale * query_peak * ROPE)
    second_key = first_key - jnp.where(rope_part[None, :], lowered * signs, 0.0)
    positions = jnp.arange(CTX)[None, :, None]
    first_hot = (positions == first_pos[:, None, None]) & in_set[None, None, :]
    second_hot = (positions == second_pos[:, None, None]) & in_set[None, None, :]
    placed = jnp.where(first_hot, first_key[:, None, :], base)
    placed = jnp.where(second_hot, second_key[:, None, :], placed)
    return placed.astype(jnp.bfloat16)


def draw_lengths(key, part):
    key = jax.random.fold_in(key, 7)
    first_key, second_key = jax.random.split(key)
    drawn = jax.random.randint(first_key, (PROMPTS,), CTX // 8, CTX + 1)
    longest = jax.random.randint(second_key, (), 0, PROMPTS)
    return drawn.at[longest].set(CTX).astype(jnp.int32)


def plant(array, stream_key, least, largest):
    longest = array.shape.index(max(array.shape))
    spots = []
    for shift in (0, 1):
        where = [jax.random.randint(jax.random.fold_in(stream_key, axis), (), 0, length) for axis, length in enumerate(array.shape)]
        where[longest] = (where[longest] + shift) % array.shape[longest]
        spots.append(tuple(where))
    return array.at[spots[0]].set(least).at[spots[1]].set(largest)


def levels(rng, shape, cuts, least, top_value):
    loudness = 1.0
    for axis_at, shards_of in cuts:
        draws = jax.random.uniform(jax.random.fold_in(jax.random.fold_in(rng, 6), axis_at), (shards_of,), jnp.float32, least / len(cuts), top_value / len(cuts))
        loudness = loudness * jnp.repeat(jnp.exp(draws), shape[axis_at] // shards_of).reshape((-1,) + (1,) * (len(shape) - 1 - axis_at))
    return loudness


def assign_block(rng, own, number, rows, count, top, reach, lean):
    order = jax.random.permutation(rng, count)
    crowded, ordinary = portions_of(count, rows * top, reach, lean, True), portions_of(count, rows * top, reach, lean, False)
    places = jnp.arange(count)

    def named(sizes, offset_by):
        used = int((sizes > 0).sum())
        fixed = max(1, used // 4)
        shifted = fixed + (places - fixed + offset_by * (used - fixed)) % max(1, count - fixed)
        return jnp.zeros((count,), jnp.int32).at[order[jnp.where(places < fixed, places, shifted)]].set(jnp.asarray(sizes, jnp.int32))

    sizes = jnp.where(number % 4 == 0, named(crowded, number // 4), named(ordinary, number - number // 4 - 1))
    mixed = jax.random.permutation(jax.random.fold_in(own, 3), count)
    donor, receiver = mixed[0:count // 2 * 2:2], mixed[1:count // 2 * 2:2]
    slack = jnp.minimum(sizes[donor] - 1, reach - sizes[receiver]) // 2
    slack = jnp.where((donor == order[0]) | (receiver == order[0]) | (sizes[receiver] == 0), 0, jnp.maximum(slack, 0))
    shifted = jax.random.randint(jax.random.fold_in(own, 4), (count // 2,), 0, 1 << 20) % (slack + 1)
    sizes = sizes.at[donor].add(-shifted).at[receiver].add(shifted)
    members = jnp.searchsorted(jnp.cumsum(sizes), jnp.arange(rows * top), side="right").astype(jnp.int32)
    listing = members.reshape(top, rows).T
    listing = listing[jax.random.permutation(jax.random.fold_in(own, 1), rows)]
    offset_by = jax.random.randint(jax.random.fold_in(own, 2), (rows, 1), 0, top)
    return jnp.take_along_axis(listing, (jnp.arange(top)[None, :] + offset_by) % top, axis=1)


def portions_of(count, total, limit, lean, full):
    weights = [(1 << 20) // math.isqrt(standing ** lean) + 1 for standing in range(1, count + 1)]
    largest = limit if full else min(limit, max(-(-total // count), total * weights[0] // sum(weights)))
    least = 1 if total - largest >= count - 1 else 0
    given, spare = [largest] + [least] * (count - 1), total - largest - least * (count - 1)
    while spare > 0:
        candidates = [i for i in range(1, count) if given[i] < largest] or [i for i in range(1, count) if given[i] < limit]
        whole, budget = sum([weights[i] for i in candidates]), spare
        for i in candidates:
            extra = min(limit - given[i], max(1, budget * weights[i] // whole), spare)
            given[i] = given[i] + extra
            spare = spare - extra
    return np.array(given)


def bell_draw(own_key, extent, scale, limit, cuts=(), held_as=jnp.bfloat16):
    factor_of = levels(own_key, extent, cuts, -0.22, 0.18) if cuts else 1.0
    array = jax.random.normal(own_key, extent, jnp.float32) * scale * factor_of
    return jnp.minimum(jnp.maximum(array, -limit), limit).astype(held_as)


def setup_inputs(seed: int = 0) -> dict:
    seeds = jax.random.split(jax.random.key(seed), 14)
    queries = draw_queries(jax.random.fold_in(seeds[13], 71), 0)
    prompt_cache = draw_prompt_cache(jax.random.fold_in(seeds[13], 71), 0)
    beam_cache = bell_draw(seeds[2], (ROWS, GEN, LAT + ROPE), 1.0, 6.0, ((0, 16),))
    new_latent = bell_draw(seeds[3], (ROWS, LAT + ROPE), 1.0, 6.0, ((0, 16),))
    parents = plant(jax.random.randint(seeds[4], (ROWS,), 0, BEAMS), jax.random.fold_in(seeds[4], 1), 0, BEAMS - 1).astype(jnp.int32)
    lengths = draw_lengths(jax.random.fold_in(seeds[13], 71), 0)
    up_values = bell_draw(seeds[6], (HEADS, LAT, VHEAD), LAT ** -0.5, 0.25, ((0, 2),))
    moe_input = bell_draw(seeds[7], (ROWS, D), 1.0, 6.0, ((0, 16), (1, 2)))
    routes_keys = jax.random.split(jax.random.fold_in(seeds[8], 1), ROWS // ROWS_DEV)
    routes_turns = jax.random.permutation(jax.random.fold_in(seeds[8], 3), ROWS // ROWS_DEV)
    routes = jax.vmap(lambda own, number: assign_block(jax.random.fold_in(seeds[8], 2), own, number, ROWS_DEV, EXPERTS, TOPK, CAP, 2))(routes_keys, routes_turns).reshape((ROWS, TOPK))
    route_scores = jnp.clip(jnp.exp(math.log(1.0) - 2.9957323 * jax.random.uniform(seeds[9], (ROWS, TOPK), jnp.float32) ** levels(seeds[9], (ROWS, TOPK), ((0, 16),), -0.2, 0.2)), 0.05, 1.0)
    w_gate = bell_draw(seeds[10], (EXPERTS, D, FF), D ** -0.5, 0.0625, ((0, 16), (2, 2)))
    w_up = bell_draw(seeds[11], (EXPERTS, D, FF), D ** -0.5, 0.0625, ((0, 16), (2, 2)))
    w_down = bell_draw(seeds[12], (EXPERTS, FF, D), FF ** -0.5, 0.125, ((0, 16), (1, 2)))
    return dict(queries=queries, prompt_cache=prompt_cache, beam_cache=beam_cache, new_latent=new_latent, parents=parents, lengths=lengths, up_values=up_values, moe_input=moe_input, routes=routes, route_scores=route_scores, w_gate=w_gate, w_up=w_up, w_down=w_down)


score_scale = 192.0 ** -0.5
neg_fill = -1.0e30


def attend_prompt(query_block, prompt_keys, beam_keys, new_keys, length):
    query_f = query_block.astype(jnp.float32)
    prompt_scores = jnp.einsum("bhc,kc->bhk", query_f, prompt_keys.astype(jnp.float32)) * score_scale
    positions = jnp.arange(prompt_keys.shape[0])
    prompt_scores = jnp.where(positions[None, None, :] < length, prompt_scores, neg_fill)
    beam_scores = jnp.einsum("bhc,bgc->bhg", query_f, beam_keys.astype(jnp.float32)) * score_scale
    new_scores = jnp.einsum("bhc,bc->bh", query_f, new_keys.astype(jnp.float32)) * score_scale
    top = jnp.maximum(jnp.maximum(jnp.max(prompt_scores, axis=-1), jnp.max(beam_scores, axis=-1)), new_scores)
    prompt_exp = jnp.exp(prompt_scores - top[..., None])
    beam_exp = jnp.exp(beam_scores - top[..., None])
    new_exp = jnp.exp(new_scores - top)
    total = jnp.sum(prompt_exp, axis=-1) + jnp.sum(beam_exp, axis=-1) + new_exp
    prompt_weight = (prompt_exp / total[..., None]).astype(jnp.bfloat16).astype(jnp.float32)
    beam_weight = (beam_exp / total[..., None]).astype(jnp.bfloat16).astype(jnp.float32)
    new_weight = (new_exp / total).astype(jnp.bfloat16).astype(jnp.float32)
    mixed = jnp.einsum("bhk,kl->bhl", prompt_weight, prompt_keys[:, :LAT].astype(jnp.float32))
    mixed = mixed + jnp.einsum("bhg,bgl->bhl", beam_weight, beam_keys[:, :, :LAT].astype(jnp.float32))
    mixed = mixed + new_weight[..., None] * new_keys[:, None, :LAT].astype(jnp.float32)
    return mixed.astype(jnp.bfloat16)


def attend_packed(packed):
    return attend_prompt(packed[0], packed[1], packed[2], packed[3], packed[4])


def reference(queries, prompt_cache, beam_cache, new_latent, parents, lengths, up_values, moe_input, routes, route_scores, w_gate, w_up, w_down):
    key_width = LAT + ROPE
    parent_rows = ((jnp.arange(ROWS) // BEAMS) * BEAMS + parents).astype(jnp.int32)
    picked = jnp.take(beam_cache, parent_rows, axis=0)
    latents = lax.map(attend_packed, (queries.reshape(PROMPTS, BEAMS, HEADS, key_width), prompt_cache, picked.reshape(PROMPTS, BEAMS, GEN, key_width), new_latent.reshape(PROMPTS, BEAMS, key_width), lengths))
    latents = latents.reshape(ROWS, HEADS, LAT)
    attn_values = jnp.einsum("rhl,hlv->rhv", latents.astype(jnp.float32), up_values.astype(jnp.float32)).astype(jnp.bfloat16).reshape(ROWS, HEADS * VHEAD)

    item_total = ROWS * TOPK
    flat_routes = routes.reshape(-1)
    bound = N_EXPERT * CAP

    def one_expert(outputs, expert_id):
        found = jnp.nonzero(flat_routes == expert_id, size=bound, fill_value=item_total)[0].astype(jnp.int32)
        row_ids = (jnp.where(found < item_total, found, 0) // TOPK).astype(jnp.int32)
        inputs = jnp.take(moe_input, row_ids, axis=0)
        gate_act = jnp.dot(inputs, w_gate[expert_id], preferred_element_type=jnp.float32)
        up_act = jnp.dot(inputs, w_up[expert_id], preferred_element_type=jnp.float32)
        hidden = (jax.nn.silu(gate_act) * up_act).astype(jnp.bfloat16)
        grouped = hidden.reshape(bound, N_ATTN, FF // N_ATTN).astype(jnp.float32)
        down_groups = w_down[expert_id].reshape(N_ATTN, FF // N_ATTN, D).astype(jnp.float32)
        partial_sums = jnp.einsum("nqf,qfd->qnd", grouped, down_groups).astype(jnp.bfloat16).astype(jnp.float32)
        result = jnp.sum(partial_sums, axis=0).astype(jnp.bfloat16)
        outputs = outputs.at[found].set(result, mode="drop")
        return outputs, None

    start = jnp.zeros((item_total, D), jnp.bfloat16)
    outputs, unused = lax.scan(one_expert, start, jnp.arange(EXPERTS).astype(jnp.int32))
    share = 2.5 * route_scores / jnp.sum(route_scores, axis=1, keepdims=True)
    moe_out = jnp.einsum("rk,rkd->rd", share, outputs.reshape(ROWS, TOPK, D).astype(jnp.float32)).astype(jnp.bfloat16)
    return attn_values, moe_out
```

```python
from functools import partial

import jax
import jax.numpy as jnp
from jax import lax
from jax.sharding import PartitionSpec as P

score_scale = 192.0 ** (-0.5)
neg_fill = -1e30


def attend_prompt(query_block, prompt_keys, beam_keys, new_keys, length, latent_width):
    prompt_scores = (
        jnp.einsum("bhc,kc->bhk", query_block, prompt_keys, preferred_element_type=jnp.float32)
        * score_scale
    )
    positions = jnp.arange(prompt_keys.shape[0])
    prompt_scores = jnp.where(positions[None, None, :] < length, prompt_scores, neg_fill)
    beam_scores = (
        jnp.einsum("bhc,bgc->bhg", query_block, beam_keys, preferred_element_type=jnp.float32)
        * score_scale
    )
    new_scores = (
        jnp.einsum("bhc,bc->bh", query_block, new_keys, preferred_element_type=jnp.float32)
        * score_scale
    )
    top = jnp.maximum(
        jnp.maximum(jnp.max(prompt_scores, axis=-1), jnp.max(beam_scores, axis=-1)), new_scores
    )
    prompt_exp = jnp.exp(prompt_scores - top[..., None])
    beam_exp = jnp.exp(beam_scores - top[..., None])
    new_exp = jnp.exp(new_scores - top)
    total = jnp.sum(prompt_exp, axis=-1) + jnp.sum(beam_exp, axis=-1) + new_exp
    prompt_weight = (prompt_exp / total[..., None]).astype(jnp.bfloat16)
    beam_weight = (beam_exp / total[..., None]).astype(jnp.bfloat16)
    new_weight = (new_exp / total).astype(jnp.bfloat16)
    mixed = jnp.einsum(
        "bhk,kl->bhl",
        prompt_weight,
        prompt_keys[:, :latent_width],
        preferred_element_type=jnp.float32,
    )
    mixed = mixed + jnp.einsum(
        "bhg,bgl->bhl",
        beam_weight,
        beam_keys[:, :, :latent_width],
        preferred_element_type=jnp.float32,
    )
    mixed = mixed + new_weight.astype(jnp.float32)[..., None] * new_keys[
        :, None, :latent_width
    ].astype(jnp.float32)
    return mixed.astype(jnp.bfloat16)


def expert_shares(routes, route_scores, experts):
    share = 2.5 * route_scores / jnp.sum(route_scores, axis=1, keepdims=True)
    hot = routes[:, :, None] == jnp.arange(experts)[None, None, :]
    return jnp.sum(jnp.where(hot, share[:, :, None], 0.0), axis=1)


def expert_block(rows, row_share, w_gate, w_up, w_down):
    gate_act = jnp.dot(rows, w_gate[0], preferred_element_type=jnp.float32)
    up_act = jnp.dot(rows, w_up[0], preferred_element_type=jnp.float32)
    hidden = (jax.nn.silu(gate_act) * up_act).astype(jnp.bfloat16)
    partial_out = jnp.dot(hidden, w_down[0], preferred_element_type=jnp.float32)
    return (partial_out * row_share[:, None]).astype(jnp.bfloat16)


def local(
    queries,
    prompt_cache,
    beam_cache,
    new_latent,
    parents,
    lengths,
    up_values,
    moe_input,
    routes,
    route_scores,
    w_gate,
    w_up,
    w_down,
):
    row_count, head_count, key_width = queries.shape
    prompt_count = prompt_cache.shape[0]
    beam_count = row_count // prompt_count
    latent_width = up_values.shape[1]
    parent_rows = jnp.arange(row_count) // beam_count * beam_count + parents
    picked = jnp.take(beam_cache, parent_rows, axis=0)
    attend = partial(attend_prompt, latent_width=latent_width)
    latents = jax.vmap(attend)(
        queries.reshape(prompt_count, beam_count, head_count, key_width),
        prompt_cache,
        picked.reshape(prompt_count, beam_count, -1, key_width),
        new_latent.reshape(prompt_count, beam_count, key_width),
        lengths,
    )
    latents = latents.reshape(row_count, head_count, latent_width)
    attn_values = (
        jnp.einsum("rhl,hlv->rhv", latents, up_values, preferred_element_type=jnp.float32)
        .astype(jnp.bfloat16)
        .reshape(row_count, -1)
    )
    experts = lax.axis_size("expert")
    shares = lax.all_gather(expert_shares(routes, route_scores, experts), "expert", axis=0, tiled=True)
    row_share = lax.dynamic_index_in_dim(shares, lax.axis_index("expert"), axis=1, keepdims=False)
    rows = lax.all_gather(moe_input, "expert", axis=0, tiled=True)
    rows = lax.all_gather(rows, "attn", axis=1, tiled=True)
    scaled = expert_block(rows, row_share, w_gate, w_up, w_down)
    halves = lax.psum_scatter(scaled, "attn", scatter_dimension=1, tiled=True)
    moe_out = lax.psum_scatter(halves, "expert", scatter_dimension=0, tiled=True)
    return (attn_values, moe_out)


def solution(mesh):
    in_specs = (
        P("expert", "attn", None),
        P("expert", None, None),
        P("expert", None, None),
        P("expert", None),
        P("expert"),
        P("expert"),
        P("attn", None, None),
        P("expert", "attn"),
        P("expert", None),
        P("expert", None),
        P("expert", None, "attn"),
        P("expert", None, "attn"),
        P("expert", "attn", None),
    )
    out_specs = (P("expert", "attn"), P("expert", "attn"))
    return jax.shard_map(local, mesh=mesh, in_specs=in_specs, out_specs=out_specs, check_vma=False)
```

```python
from functools import partial

import jax
import jax.numpy as jnp
from jax import lax
from jax.experimental import pallas as pl
from jax.experimental.pallas import tpu as pltpu
from jax.sharding import PartitionSpec as P

score_scale = 192.0 ** (-0.5)
neg_fill = -1e30


def attend_prompt(query_block, prompt_keys, beam_keys, new_keys, length, latent_width):
    prompt_scores = (
        jnp.einsum("bhc,kc->bhk", query_block, prompt_keys, preferred_element_type=jnp.float32)
        * score_scale
    )
    positions = jnp.arange(prompt_keys.shape[0])
    prompt_scores = jnp.where(positions[None, None, :] < length, prompt_scores, neg_fill)
    beam_scores = (
        jnp.einsum("bhc,bgc->bhg", query_block, beam_keys, preferred_element_type=jnp.float32)
        * score_scale
    )
    new_scores = (
        jnp.einsum("bhc,bc->bh", query_block, new_keys, preferred_element_type=jnp.float32)
        * score_scale
    )
    top = jnp.maximum(
        jnp.maximum(jnp.max(prompt_scores, axis=-1), jnp.max(beam_scores, axis=-1)), new_scores
    )
    prompt_exp = jnp.exp(prompt_scores - top[..., None])
    beam_exp = jnp.exp(beam_scores - top[..., None])
    new_exp = jnp.exp(new_scores - top)
    total = jnp.sum(prompt_exp, axis=-1) + jnp.sum(beam_exp, axis=-1) + new_exp
    prompt_weight = (prompt_exp / total[..., None]).astype(jnp.bfloat16)
    beam_weight = (beam_exp / total[..., None]).astype(jnp.bfloat16)
    new_weight = (new_exp / total).astype(jnp.bfloat16)
    mixed = jnp.einsum(
        "bhk,kl->bhl",
        prompt_weight,
        prompt_keys[:, :latent_width],
        preferred_element_type=jnp.float32,
    )
    mixed = mixed + jnp.einsum(
        "bhg,bgl->bhl",
        beam_weight,
        beam_keys[:, :, :latent_width],
        preferred_element_type=jnp.float32,
    )
    mixed = mixed + new_weight.astype(jnp.float32)[..., None] * new_keys[
        :, None, :latent_width
    ].astype(jnp.float32)
    return mixed.astype(jnp.bfloat16)


def expert_shares(routes, route_scores, experts):
    share = 2.5 * route_scores / jnp.sum(route_scores, axis=1, keepdims=True)
    hot = routes[:, :, None] == jnp.arange(experts)[None, None, :]
    return jnp.sum(jnp.where(hot, share[:, :, None], 0.0), axis=1)


def expert_block(rows, row_share, w_gate, w_up, w_down):
    gate_act = jnp.dot(rows, w_gate[0], preferred_element_type=jnp.float32)
    up_act = jnp.dot(rows, w_up[0], preferred_element_type=jnp.float32)
    hidden = (jax.nn.silu(gate_act) * up_act).astype(jnp.bfloat16)
    partial_out = jnp.dot(hidden, w_down[0], preferred_element_type=jnp.float32)
    return (partial_out * row_share[:, None]).astype(jnp.bfloat16)


class Links:
    def __init__(self, send_sem, recv_sem):
        expert = lax.axis_index("expert")
        self.z, self.y, self.c = expert // 4, expert // 2 % 2, expert % 2
        self.x = lax.axis_index("attn")
        self.sems, self.count, self.copies = (send_sem, recv_sem), 0, []

    def device(self, dz=0, fy=0, fc=0, fx=0):
        return {"expert": self.expert_at(dz, fy, fc), "attn": self.flip(self.x, fx)}

    def flip(self, value, by):
        return 1 - value if by else value

    def expert_at(self, dz=0, fy=0, fc=0):
        return ((self.z + dz) % 4 * 2 + self.flip(self.y, fy)) * 2 + self.flip(self.c, fc)

    def greet(self):
        barrier = pltpu.get_barrier_semaphore()
        others = [dict(fc=1), dict(fx=1), dict(fy=1), dict(dz=1), dict(dz=2), dict(dz=3)]
        for other in others:
            pl.semaphore_signal(
                barrier, inc=1, device_id=self.device(**other), device_id_type=pl.DeviceIdType.MESH
            )
        pl.semaphore_wait(barrier, len(others))

    def send(self, source, target, **other):
        copy = pltpu.make_async_remote_copy(
            src_ref=source,
            dst_ref=target,
            send_sem=self.sems[0].at[self.count],
            recv_sem=self.sems[1].at[self.count],
            device_id=self.device(**other),
            device_id_type=pl.DeviceIdType.MESH,
        )
        self.count += 1
        copy.start()
        self.copies.append(copy)
        return copy

    def finish(self):
        for copy in self.copies:
            copy.wait_send()


gather_copies = 62
scatter_copies = 43


def gather_kernel(x_ref, s_ref, out_ref, shares_ref, send_sem, recv_sem, local_sem):
    rows, width = x_ref.shape
    half = width // 2
    links = Links(send_sem, recv_sem)

    def block(d, fy=0, fx=0, h=None):
        row = pl.multiple_of(links.expert_at(-d, fy) * rows, rows)
        first = links.flip(links.x, fx) * width + (0 if h is None else h * half)
        return out_ref.at[
            pl.ds(row, rows), pl.ds(pl.multiple_of(first, 128), width if h is None else half)
        ]

    def share_block(d, fy=0):
        return shares_ref.at[pl.ds(pl.multiple_of(links.expert_at(-d, fy) * rows, rows), rows)]

    own = pltpu.make_async_copy(x_ref, block(0), local_sem.at[0])
    own_share = pltpu.make_async_copy(s_ref, share_block(0), local_sem.at[1])
    own.start()
    own_share.start()
    links.greet()
    order = (0, 1, 3, 2)
    by_z, by_z_share = {}, {}
    by_x, by_y, by_xy, by_yx, by_y_share, last = {}, {}, {}, {}, {}, []

    def source(d, h=None):
        if d:
            return block(d, h=h)
        return x_ref if h is None else x_ref.at[:, pl.ds(h * half, half)]

    def spread(d):
        if d:
            by_z[d].wait_recv()
        by_x[d, 0] = links.send(source(d, 0), block(d, h=0), fx=1)
        by_y[d, 1] = links.send(source(d, 1), block(d, h=1), fy=1)
        by_x[d, 1] = links.send(source(d, 1), block(d, h=1), fx=1)
        by_y[d, 0] = links.send(source(d, 0), block(d, h=0), fy=1)
        last.append(links.send(source(d), block(d), fc=1))
        if d:
            by_z_share[d].wait_recv()
        shares = share_block(d) if d else s_ref
        by_y_share[d] = links.send(shares, share_block(d), fy=1)
        last.append(links.send(shares, share_block(d), fc=1))

    def relay(d):
        by_x[d, 0].wait_recv()
        by_xy[d] = links.send(block(d, fx=1, h=0), block(d, fx=1, h=0), fy=1)
        by_y[d, 1].wait_recv()
        by_yx[d] = links.send(block(d, fy=1, h=1), block(d, fy=1, h=1), fx=1)
        by_x[d, 1].wait_recv()
        last.append(links.send(block(d, fx=1), block(d, fx=1), fc=1))
        by_y[d, 0].wait_recv()
        last.append(links.send(block(d, fy=1), block(d, fy=1), fc=1))
        by_y_share[d].wait_recv()
        last.append(links.send(share_block(d, 1), share_block(d, 1), fc=1))

    def settle(d):
        by_xy[d].wait_recv()
        last.append(links.send(block(d, 1, 1, 0), block(d, 1, 1, 0), fc=1))
        by_yx[d].wait_recv()
        last.append(links.send(block(d, 1, 1, 1), block(d, 1, 1, 1), fc=1))

    for d in (1, 3, 2):
        by_z[d] = links.send(x_ref, block(0), dz=d)
        by_z_share[d] = links.send(s_ref, share_block(0), dz=d)
    for step in range(6):
        if step < 4:
            spread(order[step])
        if 0 <= step - 1 < 4:
            relay(order[step - 1])
        if step >= 2:
            settle(order[step - 2])
    for copy in last:
        copy.wait_recv()
    own.wait()
    own_share.wait()
    links.finish()


def gather_rows(moe_input, shares):
    rows, width = moe_input.shape
    experts, groups = lax.axis_size("expert"), lax.axis_size("attn")
    return pl.pallas_call(
        gather_kernel,
        out_shape=(
            jax.ShapeDtypeStruct((experts * rows, groups * width), moe_input.dtype),
            jax.ShapeDtypeStruct((experts * rows, shares.shape[1]), shares.dtype),
        ),
        in_specs=[pl.BlockSpec(memory_space=pl.ANY)] * 2,
        out_specs=[pl.BlockSpec(memory_space=pl.ANY)] * 2,
        scratch_shapes=[
            pltpu.SemaphoreType.DMA((gather_copies,)),
            pltpu.SemaphoreType.DMA((gather_copies,)),
            pltpu.SemaphoreType.DMA((2,)),
        ],
        compiler_params=pltpu.CompilerParams(collective_id=0, has_side_effects=True),
    )(moe_input, shares)


def scatter_kernel(
    p_ref, out_ref, sums, from_x, from_y, second_x, second_y, from_z, send_sem, recv_sem
):
    rows, width = out_ref.shape
    half = width // 2
    halves = (pl.ds(0, half), pl.ds(half, half))
    links = Links(send_sem, recv_sem)
    order = (1, 3, 2, 0)
    pieces = ((1, 1), (1, 0), (0, 1), (0, 0))
    by_core, by_x, by_y, by_x2, by_y2, by_z = {}, {}, {}, {}, {}, {}

    def place(d, fx, fy, fc):
        row = pl.multiple_of(links.expert_at(d, fy, fc) * rows, rows)
        return row, links.flip(links.x, fx) * width

    def wide(*refs):
        total = refs[0].astype(jnp.float32)
        for value in refs[1:]:
            total = total + value.astype(jnp.float32)
        return total.astype(jnp.bfloat16)

    def add_core(d, fx, fy):
        by_core[d, fx, fy].wait_recv()
        row, column = place(d, fx, fy, 0)
        for h in range(2):
            first = pl.multiple_of(column + h * half, 128)
            mine = p_ref[pl.ds(row, rows), pl.ds(first, half)]
            sums[d, fx, fy, :, halves[h]] = wide(sums[d, fx, fy, :, halves[h]], mine)

    def first_hop(d):
        add_core(d, 1, 1)
        by_x[d, 1] = links.send(sums.at[d, 1, 1, :, halves[0]], from_x.at[d, 1], fx=1)
        by_y[d, 1] = links.send(sums.at[d, 1, 1, :, halves[1]], from_y.at[d, 1], fy=1)
        add_core(d, 1, 0)
        by_x[d, 0] = links.send(sums.at[d, 1, 0, :, halves[0]], from_x.at[d, 0], fx=1)
        add_core(d, 0, 1)
        by_y[d, 0] = links.send(sums.at[d, 0, 1, :, halves[1]], from_y.at[d, 0], fy=1)
        add_core(d, 0, 0)

    def second_hop(d):
        by_x[d, 1].wait_recv()
        sums[d, 0, 1, :, halves[0]] = wide(sums[d, 0, 1, :, halves[0]], from_x[d, 1])
        by_y2[d] = links.send(sums.at[d, 0, 1, :, halves[0]], second_y.at[d], fy=1)
        by_y[d, 1].wait_recv()
        sums[d, 1, 0, :, halves[1]] = wide(sums[d, 1, 0, :, halves[1]], from_y[d, 1])
        by_x2[d] = links.send(sums.at[d, 1, 0, :, halves[1]], second_x.at[d], fx=1)

    def third_hop(d):
        by_x[d, 0].wait_recv()
        by_y2[d].wait_recv()
        sums[d, 0, 0, :, halves[0]] = wide(
            sums[d, 0, 0, :, halves[0]], from_x[d, 0], second_y[d]
        )
        by_y[d, 0].wait_recv()
        by_x2[d].wait_recv()
        sums[d, 0, 0, :, halves[1]] = wide(
            sums[d, 0, 0, :, halves[1]], from_y[d, 0], second_x[d]
        )
        if d:
            by_z[d] = links.send(sums.at[d, 0, 0], from_z.at[d - 1], dz=d)

    links.greet()
    for d in order:
        for fx, fy in pieces:
            row, column = place(d, fx, fy, 1)
            by_core[d, fx, fy] = links.send(
                p_ref.at[pl.ds(row, rows), pl.ds(pl.multiple_of(column, 128), width)],
                sums.at[d, fx, fy],
                fc=1,
            )
    for step in range(6):
        if step < 4:
            first_hop(order[step])
        if 0 <= step - 1 < 4:
            second_hop(order[step - 1])
        if step >= 2:
            third_hop(order[step - 2])
    for d in (1, 3, 2):
        by_z[d].wait_recv()
    for h in range(2):
        out_ref[:, halves[h]] = wide(
            sums[0, 0, 0, :, halves[h]],
            from_z[0, :, halves[h]],
            from_z[1, :, halves[h]],
            from_z[2, :, halves[h]],
        )
    links.finish()


def scatter_rows(scaled):
    rows = scaled.shape[0] // lax.axis_size("expert")
    width = scaled.shape[1] // lax.axis_size("attn")
    kind = scaled.dtype
    return pl.pallas_call(
        scatter_kernel,
        out_shape=jax.ShapeDtypeStruct((rows, width), kind),
        in_specs=[pl.BlockSpec(memory_space=pltpu.VMEM)],
        out_specs=pl.BlockSpec(memory_space=pltpu.VMEM),
        scratch_shapes=[
            pltpu.VMEM((4, 2, 2, rows, width), kind),
            pltpu.VMEM((4, 2, rows, width // 2), kind),
            pltpu.VMEM((4, 2, rows, width // 2), kind),
            pltpu.VMEM((4, rows, width // 2), kind),
            pltpu.VMEM((4, rows, width // 2), kind),
            pltpu.VMEM((3, rows, width), kind),
            pltpu.SemaphoreType.DMA((scatter_copies,)),
            pltpu.SemaphoreType.DMA((scatter_copies,)),
        ],
        compiler_params=pltpu.CompilerParams(
            collective_id=1, has_side_effects=True, vmem_limit_bytes=40 * 1024 * 1024
        ),
    )(scaled)


def local(
    queries,
    prompt_cache,
    beam_cache,
    new_latent,
    parents,
    lengths,
    up_values,
    moe_input,
    routes,
    route_scores,
    w_gate,
    w_up,
    w_down,
):
    row_count, head_count, key_width = queries.shape
    prompt_count = prompt_cache.shape[0]
    beam_count = row_count // prompt_count
    latent_width = up_values.shape[1]
    parent_rows = jnp.arange(row_count) // beam_count * beam_count + parents
    picked = jnp.take(beam_cache, parent_rows, axis=0)
    attend = partial(attend_prompt, latent_width=latent_width)
    latents = jax.vmap(attend)(
        queries.reshape(prompt_count, beam_count, head_count, key_width),
        prompt_cache,
        picked.reshape(prompt_count, beam_count, -1, key_width),
        new_latent.reshape(prompt_count, beam_count, key_width),
        lengths,
    )
    latents = latents.reshape(row_count, head_count, latent_width)
    attn_values = (
        jnp.einsum("rhl,hlv->rhv", latents, up_values, preferred_element_type=jnp.float32)
        .astype(jnp.bfloat16)
        .reshape(row_count, -1)
    )
    experts = lax.axis_size("expert")
    own_shares = expert_shares(routes, route_scores, experts)
    on_grid = experts == 16 and lax.axis_size("attn") == 2
    if on_grid:
        own_shares = jnp.pad(own_shares, ((0, 0), (0, 128 - experts)))
        rows, shares = gather_rows(moe_input, own_shares)
    else:
        shares = lax.all_gather(own_shares, "expert", axis=0, tiled=True)
        rows = lax.all_gather(moe_input, "expert", axis=0, tiled=True)
        rows = lax.all_gather(rows, "attn", axis=1, tiled=True)
    row_share = lax.dynamic_index_in_dim(shares, lax.axis_index("expert"), axis=1, keepdims=False)
    scaled = expert_block(rows, row_share, w_gate, w_up, w_down)
    if on_grid:
        moe_out = scatter_rows(scaled)
    else:
        halves = lax.psum_scatter(scaled, "attn", scatter_dimension=1, tiled=True)
        moe_out = lax.psum_scatter(halves, "expert", scatter_dimension=0, tiled=True)
    return (attn_values, moe_out)


def solution(mesh):
    in_specs = (
        P("expert", "attn", None),
        P("expert", None, None),
        P("expert", None, None),
        P("expert", None),
        P("expert"),
        P("expert"),
        P("attn", None, None),
        P("expert", "attn"),
        P("expert", None),
        P("expert", None),
        P("expert", None, "attn"),
        P("expert", None, "attn"),
        P("expert", "attn", None),
    )
    out_specs = (P("expert", "attn"), P("expert", "attn"))
    return jax.shard_map(local, mesh=mesh, in_specs=in_specs, out_specs=out_specs, check_vma=False)
```

```python
from functools import partial

import jax
import jax.numpy as jnp
from jax import lax
from jax.experimental import pallas as pl
from jax.experimental.pallas import tpu as pltpu
from jax.sharding import PartitionSpec as P

score_scale = 192.0 ** (-0.5)
neg_fill = -1e30


def attend_prompt(query_block, prompt_keys, beam_keys, new_keys, length, latent_width):
    prompt_scores = (
        jnp.einsum("bhc,kc->bhk", query_block, prompt_keys, preferred_element_type=jnp.float32)
        * score_scale
    )
    positions = jnp.arange(prompt_keys.shape[0])
    prompt_scores = jnp.where(positions[None, None, :] < length, prompt_scores, neg_fill)
    beam_scores = (
        jnp.einsum("bhc,bgc->bhg", query_block, beam_keys, preferred_element_type=jnp.float32)
        * score_scale
    )
    new_scores = (
        jnp.einsum("bhc,bc->bh", query_block, new_keys, preferred_element_type=jnp.float32)
        * score_scale
    )
    top = jnp.maximum(
        jnp.maximum(jnp.max(prompt_scores, axis=-1), jnp.max(beam_scores, axis=-1)), new_scores
    )
    prompt_exp = jnp.exp(prompt_scores - top[..., None])
    beam_exp = jnp.exp(beam_scores - top[..., None])
    new_exp = jnp.exp(new_scores - top)
    total = jnp.sum(prompt_exp, axis=-1) + jnp.sum(beam_exp, axis=-1) + new_exp
    prompt_weight = (prompt_exp / total[..., None]).astype(jnp.bfloat16)
    beam_weight = (beam_exp / total[..., None]).astype(jnp.bfloat16)
    new_weight = (new_exp / total).astype(jnp.bfloat16)
    mixed = jnp.einsum(
        "bhk,kl->bhl",
        prompt_weight,
        prompt_keys[:, :latent_width],
        preferred_element_type=jnp.float32,
    )
    mixed = mixed + jnp.einsum(
        "bhg,bgl->bhl",
        beam_weight,
        beam_keys[:, :, :latent_width],
        preferred_element_type=jnp.float32,
    )
    mixed = mixed + new_weight.astype(jnp.float32)[..., None] * new_keys[
        :, None, :latent_width
    ].astype(jnp.float32)
    return mixed.astype(jnp.bfloat16)


def expert_shares(routes, route_scores, experts):
    share = 2.5 * route_scores / jnp.sum(route_scores, axis=1, keepdims=True)
    hot = routes[:, :, None] == jnp.arange(experts)[None, None, :]
    return jnp.sum(jnp.where(hot, share[:, :, None], 0.0), axis=1)


def expert_block(rows, row_share, w_gate, w_up, w_down):
    gate_act = jnp.dot(rows, w_gate[0], preferred_element_type=jnp.float32)
    up_act = jnp.dot(rows, w_up[0], preferred_element_type=jnp.float32)
    hidden = (jax.nn.silu(gate_act) * up_act).astype(jnp.bfloat16)
    partial_out = jnp.dot(hidden, w_down[0], preferred_element_type=jnp.float32)
    return (partial_out * row_share[:, None]).astype(jnp.bfloat16)


class Links:
    def __init__(self, send_sem, recv_sem):
        expert = lax.axis_index("expert")
        self.z, self.y, self.c = expert // 4, expert // 2 % 2, expert % 2
        self.x = lax.axis_index("attn")
        self.sems, self.count, self.copies = (send_sem, recv_sem), 0, []

    def device(self, dz=0, fy=0, fc=0, fx=0):
        return {"expert": self.expert_at(dz, fy, fc), "attn": self.flip(self.x, fx)}

    def flip(self, value, by):
        return 1 - value if by else value

    def expert_at(self, dz=0, fy=0, fc=0):
        return ((self.z + dz + 4) % 4 * 2 + self.flip(self.y, fy)) * 2 + self.flip(self.c, fc)

    def greet(self):
        barrier = pltpu.get_barrier_semaphore()
        others = [dict(fc=1), dict(fx=1), dict(fy=1), dict(dz=1), dict(dz=2), dict(dz=3)]
        for other in others:
            pl.semaphore_signal(
                barrier, inc=1, device_id=self.device(**other), device_id_type=pl.DeviceIdType.MESH
            )
        pl.semaphore_wait(barrier, len(others))

    def send(self, source, target, **other):
        copy = pltpu.make_async_remote_copy(
            src_ref=source,
            dst_ref=target,
            send_sem=self.sems[0].at[self.count],
            recv_sem=self.sems[1].at[self.count],
            device_id=self.device(**other),
            device_id_type=pl.DeviceIdType.MESH,
        )
        self.count += 1
        copy.start()
        self.copies.append(copy)
        return copy

    def finish(self):
        for copy in self.copies:
            copy.wait_send()


gather_copies = 62
scatter_copies = 43


def gather_kernel(
    experts, x_ref, routes_ref, scores_ref, gate_ref, up_ref, hidden_ref, shares_ref,
    out_ref, gate_held, up_held, send_sem, recv_sem, local_sem
):
    rows, width = x_ref.shape
    half = width // 2
    links = Links(send_sem, recv_sem)

    def block(d, fy=0, fx=0, h=None):
        row = pl.multiple_of(links.expert_at(-d, fy) * rows, rows)
        first = links.flip(links.x, fx) * width + (0 if h is None else h * half)
        return out_ref.at[
            pl.ds(row, rows), pl.ds(pl.multiple_of(first, 128), width if h is None else half)
        ]

    def share_block(d, fy=0):
        return shares_ref.at[pl.ds(pl.multiple_of(links.expert_at(-d, fy) * rows, rows), rows)]

    own = pltpu.make_async_copy(x_ref, block(0), local_sem.at[0])
    gate_copy = pltpu.make_async_copy(gate_ref.at[0], gate_held, local_sem.at[1])
    up_copy = pltpu.make_async_copy(up_ref.at[0], up_held, local_sem.at[2])
    own.start()
    gate_copy.start()
    up_copy.start()
    lanes = lax.broadcasted_iota(jnp.int32, (rows, shares_ref.shape[1]), 1)
    scores = scores_ref[...]
    share = 2.5 * scores / jnp.sum(scores, axis=1, keepdims=True)
    own_share = jnp.zeros(lanes.shape, jnp.float32)
    for k in range(scores.shape[1]):
        own_share = own_share + jnp.where(lanes == routes_ref[:, k : k + 1], share[:, k : k + 1], 0.0)
    shares_ref[pl.ds(pl.multiple_of(links.expert_at() * rows, rows), rows), :] = own_share
    links.greet()
    order = (0, 1, 3, 2)
    by_z, by_z_share = {}, {}
    by_x, by_y, by_xy, by_yx, by_y_share = {}, {}, {}, {}, {}
    last = {d: [] for d in order}

    def source(d, h=None):
        if d:
            return block(d, h=h)
        return x_ref if h is None else x_ref.at[:, pl.ds(h * half, half)]

    def spread(d):
        if d:
            by_z[d].wait_recv()
        by_x[d, 0] = links.send(source(d, 0), block(d, h=0), fx=1)
        by_y[d, 1] = links.send(source(d, 1), block(d, h=1), fy=1)
        by_x[d, 1] = links.send(source(d, 1), block(d, h=1), fx=1)
        by_y[d, 0] = links.send(source(d, 0), block(d, h=0), fy=1)
        last[d].append(links.send(source(d), block(d), fc=1))
        if d:
            by_z_share[d].wait_recv()
        shares = share_block(d)
        by_y_share[d] = links.send(shares, share_block(d), fy=1)
        last[d].append(links.send(shares, share_block(d), fc=1))

    def relay(d):
        by_x[d, 0].wait_recv()
        by_xy[d] = links.send(block(d, fx=1, h=0), block(d, fx=1, h=0), fy=1)
        by_y[d, 1].wait_recv()
        by_yx[d] = links.send(block(d, fy=1, h=1), block(d, fy=1, h=1), fx=1)
        by_x[d, 1].wait_recv()
        last[d].append(links.send(block(d, fx=1), block(d, fx=1), fc=1))
        by_y[d, 0].wait_recv()
        last[d].append(links.send(block(d, fy=1), block(d, fy=1), fc=1))
        by_y_share[d].wait_recv()
        last[d].append(links.send(share_block(d, 1), share_block(d, 1), fc=1))

    def settle(d):
        by_xy[d].wait_recv()
        last[d].append(links.send(block(d, 1, 1, 0), block(d, 1, 1, 0), fc=1))
        by_yx[d].wait_recv()
        last[d].append(links.send(block(d, 1, 1, 1), block(d, 1, 1, 1), fc=1))

    def compute(d):
        if d == 0:
            own.wait()
            gate_copy.wait()
            up_copy.wait()
        for copy in last[d]:
            copy.wait_recv()
        group = pl.ds(pl.multiple_of((links.z - d + 4) % 4 * (4 * rows), 4 * rows), 4 * rows)

        @pl.loop(0, hidden_ref.shape[1] // 256)
        def _(tile):
            columns = pl.ds(pl.multiple_of(tile * 256, 256), 256)
            gate = jnp.dot(out_ref[group, :], gate_held[:, columns], preferred_element_type=jnp.float32)
            up = jnp.dot(out_ref[group, :], up_held[:, columns], preferred_element_type=jnp.float32)
            hidden_ref[group, columns] = (jax.nn.silu(gate) * up).astype(hidden_ref.dtype)

    for d in (1, 3, 2):
        by_z[d] = links.send(x_ref, block(0), dz=d)
        by_z_share[d] = links.send(share_block(0), share_block(0), dz=d)
    for step in range(6):
        if step < 4:
            spread(order[step])
        if 0 <= step - 1 < 4:
            relay(order[step - 1])
        if step >= 3:
            compute(order[step - 3])
        if step >= 2:
            settle(order[step - 2])
    compute(order[3])
    links.finish()


def gather_rows(moe_input, routes, route_scores, w_gate, w_up):
    rows, width = moe_input.shape
    experts, groups = lax.axis_size("expert"), lax.axis_size("attn")
    kind, units = moe_input.dtype, w_gate.shape[2]
    return pl.pallas_call(
        partial(gather_kernel, experts),
        out_shape=(
            jax.ShapeDtypeStruct((experts * rows, units), kind),
            jax.ShapeDtypeStruct((experts * rows, 128), jnp.float32),
        ),
        in_specs=[pl.BlockSpec(memory_space=pltpu.VMEM)] * 3
        + [pl.BlockSpec(memory_space=pl.ANY)] * 2,
        out_specs=[pl.BlockSpec(memory_space=pltpu.VMEM)] * 2,
        scratch_shapes=[
            pltpu.VMEM((experts * rows, groups * width), kind),
            pltpu.VMEM(w_gate.shape[1:], kind),
            pltpu.VMEM(w_up.shape[1:], kind),
            pltpu.SemaphoreType.DMA((gather_copies,)),
            pltpu.SemaphoreType.DMA((gather_copies,)),
            pltpu.SemaphoreType.DMA((3,)),
        ],
        compiler_params=pltpu.CompilerParams(
            collective_id=0, has_side_effects=True, vmem_limit_bytes=54 * 1024 * 1024
        ),
    )(moe_input, routes, route_scores, w_gate, w_up)


def scatter_kernel(
    hidden_ref, shares_ref, down_ref, out_ref, p_ref, down_held,
    sums, from_x, from_y, second_x, second_y, from_z, send_sem, recv_sem, local_sem
):
    rows, width = out_ref.shape
    half = width // 2
    halves = (pl.ds(0, half), pl.ds(half, half))
    links = Links(send_sem, recv_sem)
    order = (1, 3, 2, 0)
    pieces = ((1, 1), (1, 0), (0, 1), (0, 0))
    by_core, by_x, by_y, by_x2, by_y2, by_z = {}, {}, {}, {}, {}, {}

    def place(d, fx, fy, fc):
        row = pl.multiple_of(links.expert_at(d, fy, fc) * rows, rows)
        return row, links.flip(links.x, fx) * width

    def wide(*refs):
        total = refs[0].astype(jnp.float32)
        for value in refs[1:]:
            total = total + value.astype(jnp.float32)
        return total.astype(jnp.bfloat16)

    def add_core(d, fx, fy):
        by_core[d, fx, fy].wait_recv()
        row, column = place(d, fx, fy, 0)
        for h in range(2):
            first = pl.multiple_of(column + h * half, 128)
            mine = p_ref[pl.ds(row, rows), pl.ds(first, half)]
            sums[d, fx, fy, :, halves[h]] = wide(sums[d, fx, fy, :, halves[h]], mine)

    def first_hop(d):
        add_core(d, 1, 1)
        by_x[d, 1] = links.send(sums.at[d, 1, 1, :, halves[0]], from_x.at[d, 1], fx=1)
        by_y[d, 1] = links.send(sums.at[d, 1, 1, :, halves[1]], from_y.at[d, 1], fy=1)
        add_core(d, 1, 0)
        by_x[d, 0] = links.send(sums.at[d, 1, 0, :, halves[0]], from_x.at[d, 0], fx=1)
        add_core(d, 0, 1)
        by_y[d, 0] = links.send(sums.at[d, 0, 1, :, halves[1]], from_y.at[d, 0], fy=1)
        add_core(d, 0, 0)

    def second_hop(d):
        by_x[d, 1].wait_recv()
        sums[d, 0, 1, :, halves[0]] = wide(sums[d, 0, 1, :, halves[0]], from_x[d, 1])
        by_y2[d] = links.send(sums.at[d, 0, 1, :, halves[0]], second_y.at[d], fy=1)
        by_y[d, 1].wait_recv()
        sums[d, 1, 0, :, halves[1]] = wide(sums[d, 1, 0, :, halves[1]], from_y[d, 1])
        by_x2[d] = links.send(sums.at[d, 1, 0, :, halves[1]], second_x.at[d], fx=1)

    def third_hop(d):
        by_x[d, 0].wait_recv()
        by_y2[d].wait_recv()
        sums[d, 0, 0, :, halves[0]] = wide(
            sums[d, 0, 0, :, halves[0]], from_x[d, 0], second_y[d]
        )
        by_y[d, 0].wait_recv()
        by_x2[d].wait_recv()
        sums[d, 0, 0, :, halves[1]] = wide(
            sums[d, 0, 0, :, halves[1]], from_y[d, 0], second_x[d]
        )
        if d:
            by_z[d] = links.send(sums.at[d, 0, 0], from_z.at[d - 1], dz=d)

    parts = [pl.ds(part * half, half) for part in range(4)]
    loads = [
        pltpu.make_async_copy(
            down_ref.at[0, :, parts[part]], down_held.at[:, parts[part]], local_sem.at[part]
        )
        for part in range(4)
    ]

    def produce(d):
        group = pl.ds(pl.multiple_of((links.z + d) % 4 * (4 * rows), 4 * rows), 4 * rows)
        shares = shares_ref[group, :]
        lanes = lax.broadcasted_iota(jnp.int32, shares.shape, 1)
        share = jnp.sum(
            jnp.where(lanes == lax.axis_index("expert"), shares, 0.0), axis=1, keepdims=True
        )
        for part in range(4):
            if d == order[0]:
                loads[part].wait()

            @pl.loop(0, half // 256)
            def _(tile):
                columns = pl.ds(pl.multiple_of(part * half + tile * 256, 256), 256)
                product = jnp.dot(
                    hidden_ref[group, :], down_held[:, columns], preferred_element_type=jnp.float32
                )
                p_ref[group, columns] = (product * share).astype(p_ref.dtype)

        for fx, fy in pieces:
            row, column = place(d, fx, fy, 1)
            by_core[d, fx, fy] = links.send(
                p_ref.at[pl.ds(row, rows), pl.ds(pl.multiple_of(column, 128), width)],
                sums.at[d, fx, fy],
                fc=1,
            )

    for load in loads:
        load.start()
    links.greet()
    produce(order[0])
    for step in range(6):
        if step + 1 < 4:
            produce(order[step + 1])
        if step < 4:
            first_hop(order[step])
        if 0 <= step - 1 < 4:
            second_hop(order[step - 1])
        if step >= 2:
            third_hop(order[step - 2])
    for d in (1, 3, 2):
        by_z[d].wait_recv()
    for h in range(2):
        out_ref[:, halves[h]] = wide(
            sums[0, 0, 0, :, halves[h]],
            from_z[0, :, halves[h]],
            from_z[1, :, halves[h]],
            from_z[2, :, halves[h]],
        )
    links.finish()


def scatter_rows(hidden, shares, w_down):
    count, full = hidden.shape[0], w_down.shape[2]
    rows, width = count // lax.axis_size("expert"), full // lax.axis_size("attn")
    kind = hidden.dtype
    return pl.pallas_call(
        scatter_kernel,
        out_shape=jax.ShapeDtypeStruct((rows, width), kind),
        in_specs=[
            pl.BlockSpec(memory_space=pltpu.VMEM),
            pl.BlockSpec(memory_space=pltpu.VMEM),
            pl.BlockSpec(memory_space=pl.ANY),
        ],
        out_specs=pl.BlockSpec(memory_space=pltpu.VMEM),
        scratch_shapes=[
            pltpu.VMEM((count, full), kind),
            pltpu.VMEM(w_down.shape[1:], kind),
            pltpu.VMEM((4, 2, 2, rows, width), kind),
            pltpu.VMEM((4, 2, rows, width // 2), kind),
            pltpu.VMEM((4, 2, rows, width // 2), kind),
            pltpu.VMEM((4, rows, width // 2), kind),
            pltpu.VMEM((4, rows, width // 2), kind),
            pltpu.VMEM((3, rows, width), kind),
            pltpu.SemaphoreType.DMA((scatter_copies,)),
            pltpu.SemaphoreType.DMA((scatter_copies,)),
            pltpu.SemaphoreType.DMA((4,)),
        ],
        compiler_params=pltpu.CompilerParams(
            collective_id=1, has_side_effects=True, vmem_limit_bytes=48 * 1024 * 1024
        ),
    )(hidden, shares, w_down)


def local(
    queries,
    prompt_cache,
    beam_cache,
    new_latent,
    parents,
    lengths,
    up_values,
    moe_input,
    routes,
    route_scores,
    w_gate,
    w_up,
    w_down,
):
    row_count, head_count, key_width = queries.shape
    prompt_count = prompt_cache.shape[0]
    beam_count = row_count // prompt_count
    latent_width = up_values.shape[1]
    parent_rows = jnp.arange(row_count) // beam_count * beam_count + parents
    picked = jnp.take(beam_cache, parent_rows, axis=0)
    attend = partial(attend_prompt, latent_width=latent_width)
    latents = jax.vmap(attend)(
        queries.reshape(prompt_count, beam_count, head_count, key_width),
        prompt_cache,
        picked.reshape(prompt_count, beam_count, -1, key_width),
        new_latent.reshape(prompt_count, beam_count, key_width),
        lengths,
    )
    latents = latents.reshape(row_count, head_count, latent_width)
    attn_values = (
        jnp.einsum("rhl,hlv->rhv", latents, up_values, preferred_element_type=jnp.float32)
        .astype(jnp.bfloat16)
        .reshape(row_count, -1)
    )
    experts = lax.axis_size("expert")
    if experts == 16 and lax.axis_size("attn") == 2:
        hidden, shares = gather_rows(moe_input, routes, route_scores, w_gate, w_up)
        moe_out = scatter_rows(hidden, shares, w_down)
    else:
        own_shares = expert_shares(routes, route_scores, experts)
        shares = lax.all_gather(own_shares, "expert", axis=0, tiled=True)
        rows = lax.all_gather(moe_input, "expert", axis=0, tiled=True)
        rows = lax.all_gather(rows, "attn", axis=1, tiled=True)
        row_share = lax.dynamic_index_in_dim(
            shares, lax.axis_index("expert"), axis=1, keepdims=False
        )
        scaled = expert_block(rows, row_share, w_gate, w_up, w_down)
        halves = lax.psum_scatter(scaled, "attn", scatter_dimension=1, tiled=True)
        moe_out = lax.psum_scatter(halves, "expert", scatter_dimension=0, tiled=True)
    return (attn_values, moe_out)


def solution(mesh):
    in_specs = (
        P("expert", "attn", None),
        P("expert", None, None),
        P("expert", None, None),
        P("expert", None),
        P("expert"),
        P("expert"),
        P("attn", None, None),
        P("expert", "attn"),
        P("expert", None),
        P("expert", None),
        P("expert", None, "attn"),
        P("expert", None, "attn"),
        P("expert", "attn", None),
    )
    out_specs = (P("expert", "attn"), P("expert", "attn"))
    return jax.shard_map(local, mesh=mesh, in_specs=in_specs, out_specs=out_specs, check_vma=False)
```

```python
from functools import partial

import jax
import jax.numpy as jnp
from jax import lax
from jax.experimental import pallas as pl
from jax.experimental.pallas import tpu as pltpu
from jax.sharding import PartitionSpec as P

score_scale = 192.0 ** (-0.5)
neg_fill = -1e30


def attend_prompt(query_block, prompt_keys, beam_keys, new_keys, length, latent_width):
    prompt_scores = (
        jnp.einsum("bhc,kc->bhk", query_block, prompt_keys, preferred_element_type=jnp.float32)
        * score_scale
    )
    positions = jnp.arange(prompt_keys.shape[0])
    prompt_scores = jnp.where(positions[None, None, :] < length, prompt_scores, neg_fill)
    beam_scores = (
        jnp.einsum("bhc,bgc->bhg", query_block, beam_keys, preferred_element_type=jnp.float32)
        * score_scale
    )
    new_scores = (
        jnp.einsum("bhc,bc->bh", query_block, new_keys, preferred_element_type=jnp.float32)
        * score_scale
    )
    top = jnp.maximum(
        jnp.maximum(jnp.max(prompt_scores, axis=-1), jnp.max(beam_scores, axis=-1)), new_scores
    )
    prompt_exp = jnp.exp(prompt_scores - top[..., None])
    beam_exp = jnp.exp(beam_scores - top[..., None])
    new_exp = jnp.exp(new_scores - top)
    total = jnp.sum(prompt_exp, axis=-1) + jnp.sum(beam_exp, axis=-1) + new_exp
    prompt_weight = (prompt_exp / total[..., None]).astype(jnp.bfloat16)
    beam_weight = (beam_exp / total[..., None]).astype(jnp.bfloat16)
    new_weight = (new_exp / total).astype(jnp.bfloat16)
    mixed = jnp.einsum(
        "bhk,kl->bhl",
        prompt_weight,
        prompt_keys[:, :latent_width],
        preferred_element_type=jnp.float32,
    )
    mixed = mixed + jnp.einsum(
        "bhg,bgl->bhl",
        beam_weight,
        beam_keys[:, :, :latent_width],
        preferred_element_type=jnp.float32,
    )
    mixed = mixed + new_weight.astype(jnp.float32)[..., None] * new_keys[
        :, None, :latent_width
    ].astype(jnp.float32)
    return mixed.astype(jnp.bfloat16)


def expert_shares(routes, route_scores, experts):
    share = 2.5 * route_scores / jnp.sum(route_scores, axis=1, keepdims=True)
    hot = routes[:, :, None] == jnp.arange(experts)[None, None, :]
    return jnp.sum(jnp.where(hot, share[:, :, None], 0.0), axis=1)


def expert_block(rows, row_share, w_gate, w_up, w_down):
    gate_act = jnp.dot(rows, w_gate[0], preferred_element_type=jnp.float32)
    up_act = jnp.dot(rows, w_up[0], preferred_element_type=jnp.float32)
    hidden = (jax.nn.silu(gate_act) * up_act).astype(jnp.bfloat16)
    partial_out = jnp.dot(hidden, w_down[0], preferred_element_type=jnp.float32)
    return (partial_out * row_share[:, None]).astype(jnp.bfloat16)


class Links:
    def __init__(self, send_sem, recv_sem):
        expert = lax.axis_index("expert")
        self.z, self.y, self.c = expert // 4, expert // 2 % 2, expert % 2
        self.x = lax.axis_index("attn")
        self.sems, self.count, self.copies = (send_sem, recv_sem), 0, []

    def device(self, dz=0, fy=0, fc=0, fx=0):
        return {"expert": self.expert_at(dz, fy, fc), "attn": self.flip(self.x, fx)}

    def flip(self, value, by):
        return 1 - value if by else value

    def expert_at(self, dz=0, fy=0, fc=0):
        return ((self.z + dz + 4) % 4 * 2 + self.flip(self.y, fy)) * 2 + self.flip(self.c, fc)

    def greet(self):
        barrier = pltpu.get_barrier_semaphore()
        others = [dict(fc=1), dict(fx=1), dict(fy=1), dict(dz=1), dict(dz=2), dict(dz=3)]
        for other in others:
            pl.semaphore_signal(
                barrier, inc=1, device_id=self.device(**other), device_id_type=pl.DeviceIdType.MESH
            )
        pl.semaphore_wait(barrier, len(others))

    def send(self, source, target, **other):
        copy = pltpu.make_async_remote_copy(
            src_ref=source,
            dst_ref=target,
            send_sem=self.sems[0].at[self.count],
            recv_sem=self.sems[1].at[self.count],
            device_id=self.device(**other),
            device_id_type=pl.DeviceIdType.MESH,
        )
        self.count += 1
        copy.start()
        self.copies.append(copy)
        return copy

    def finish(self):
        for copy in self.copies:
            copy.wait_send()


gather_copies = 62
scatter_copies = 59


def gather_kernel(
    experts, x_ref, routes_ref, scores_ref, gate_ref, up_ref, hidden_ref, shares_ref,
    out_ref, gate_held, up_held, send_sem, recv_sem, local_sem
):
    rows, width = x_ref.shape
    half = width // 2
    links = Links(send_sem, recv_sem)

    def block(d, fy=0, fx=0, h=None):
        row = pl.multiple_of(links.expert_at(-d, fy) * rows, rows)
        first = links.flip(links.x, fx) * width + (0 if h is None else h * half)
        return out_ref.at[
            pl.ds(row, rows), pl.ds(pl.multiple_of(first, 128), width if h is None else half)
        ]

    def share_block(d, fy=0):
        return shares_ref.at[pl.ds(pl.multiple_of(links.expert_at(-d, fy) * rows, rows), rows)]

    own = pltpu.make_async_copy(x_ref, block(0), local_sem.at[0])
    gate_copy = pltpu.make_async_copy(gate_ref.at[0], gate_held, local_sem.at[1])
    up_copy = pltpu.make_async_copy(up_ref.at[0], up_held, local_sem.at[2])
    own.start()
    gate_copy.start()
    up_copy.start()
    lanes = lax.broadcasted_iota(jnp.int32, (rows, shares_ref.shape[1]), 1)
    scores = scores_ref[...]
    share = 2.5 * scores / jnp.sum(scores, axis=1, keepdims=True)
    own_share = jnp.zeros(lanes.shape, jnp.float32)
    for k in range(scores.shape[1]):
        own_share = own_share + jnp.where(lanes == routes_ref[:, k : k + 1], share[:, k : k + 1], 0.0)
    shares_ref[pl.ds(pl.multiple_of(links.expert_at() * rows, rows), rows), :] = own_share
    links.greet()
    order = (0, 1, 3, 2)
    by_z, by_z_share = {}, {}
    by_x, by_y, by_xy, by_yx, by_y_share = {}, {}, {}, {}, {}
    last = {d: [] for d in order}

    def source(d, h=None):
        if d:
            return block(d, h=h)
        return x_ref if h is None else x_ref.at[:, pl.ds(h * half, half)]

    def spread(d):
        if d:
            by_z[d].wait_recv()
        by_x[d, 0] = links.send(source(d, 0), block(d, h=0), fx=1)
        by_y[d, 1] = links.send(source(d, 1), block(d, h=1), fy=1)
        by_x[d, 1] = links.send(source(d, 1), block(d, h=1), fx=1)
        by_y[d, 0] = links.send(source(d, 0), block(d, h=0), fy=1)
        last[d].append(links.send(source(d), block(d), fc=1))
        if d:
            by_z_share[d].wait_recv()
        shares = share_block(d)
        by_y_share[d] = links.send(shares, share_block(d), fy=1)
        last[d].append(links.send(shares, share_block(d), fc=1))

    def relay(d):
        by_x[d, 0].wait_recv()
        by_xy[d] = links.send(block(d, fx=1, h=0), block(d, fx=1, h=0), fy=1)
        by_y[d, 1].wait_recv()
        by_yx[d] = links.send(block(d, fy=1, h=1), block(d, fy=1, h=1), fx=1)
        by_x[d, 1].wait_recv()
        last[d].append(links.send(block(d, fx=1), block(d, fx=1), fc=1))
        by_y[d, 0].wait_recv()
        last[d].append(links.send(block(d, fy=1), block(d, fy=1), fc=1))
        by_y_share[d].wait_recv()
        last[d].append(links.send(share_block(d, 1), share_block(d, 1), fc=1))

    def settle(d):
        by_xy[d].wait_recv()
        last[d].append(links.send(block(d, 1, 1, 0), block(d, 1, 1, 0), fc=1))
        by_yx[d].wait_recv()
        last[d].append(links.send(block(d, 1, 1, 1), block(d, 1, 1, 1), fc=1))

    def compute(d):
        if d == 0:
            own.wait()
            gate_copy.wait()
            up_copy.wait()
        for copy in last[d]:
            copy.wait_recv()
        group = pl.ds(pl.multiple_of((links.z - d + 4) % 4 * (4 * rows), 4 * rows), 4 * rows)

        @pl.loop(0, hidden_ref.shape[1] // 256)
        def _(tile):
            columns = pl.ds(pl.multiple_of(tile * 256, 256), 256)
            gate = jnp.dot(out_ref[group, :], gate_held[:, columns], preferred_element_type=jnp.float32)
            up = jnp.dot(out_ref[group, :], up_held[:, columns], preferred_element_type=jnp.float32)
            hidden_ref[group, columns] = (jax.nn.silu(gate) * up).astype(hidden_ref.dtype)

    for d in (1, 3, 2):
        by_z[d] = links.send(x_ref, block(0), dz=d)
        by_z_share[d] = links.send(share_block(0), share_block(0), dz=d)
    for step in range(6):
        if step < 4:
            spread(order[step])
        if 0 <= step - 1 < 4:
            relay(order[step - 1])
        if step >= 3:
            compute(order[step - 3])
        if step >= 2:
            settle(order[step - 2])
    compute(order[3])
    links.finish()


def gather_rows(moe_input, routes, route_scores, w_gate, w_up):
    rows, width = moe_input.shape
    experts, groups = lax.axis_size("expert"), lax.axis_size("attn")
    kind, units = moe_input.dtype, w_gate.shape[2]
    return pl.pallas_call(
        partial(gather_kernel, experts),
        out_shape=(
            jax.ShapeDtypeStruct((experts * rows, units), kind),
            jax.ShapeDtypeStruct((experts * rows, 128), jnp.float32),
        ),
        in_specs=[pl.BlockSpec(memory_space=pltpu.VMEM)] * 3
        + [pl.BlockSpec(memory_space=pl.ANY)] * 2,
        out_specs=[pl.BlockSpec(memory_space=pltpu.VMEM)] * 2,
        scratch_shapes=[
            pltpu.VMEM((experts * rows, groups * width), kind),
            pltpu.VMEM(w_gate.shape[1:], kind),
            pltpu.VMEM(w_up.shape[1:], kind),
            pltpu.SemaphoreType.DMA((gather_copies,)),
            pltpu.SemaphoreType.DMA((gather_copies,)),
            pltpu.SemaphoreType.DMA((3,)),
        ],
        compiler_params=pltpu.CompilerParams(
            collective_id=0, has_side_effects=True, vmem_limit_bytes=54 * 1024 * 1024
        ),
    )(moe_input, routes, route_scores, w_gate, w_up)


def scatter_kernel(
    hidden_ref, shares_ref, down_ref, out_ref, p_ref, down_held,
    sums, from_x, from_y, second_x, second_y, from_z, send_sem, recv_sem, local_sem
):
    rows, width = out_ref.shape
    half = width // 2
    halves = (pl.ds(0, half), pl.ds(half, half))
    links = Links(send_sem, recv_sem)
    order = (1, 3, 2, 0)
    by_core, by_x, by_y, by_x2, by_y2, by_z = {}, {}, {}, {}, {}, {}

    def place(d, fx, fy, fc):
        row = pl.multiple_of(links.expert_at(d, fy, fc) * rows, rows)
        return row, links.flip(links.x, fx) * width

    def wide(*refs):
        total = refs[0].astype(jnp.float32)
        for value in refs[1:]:
            total = total + value.astype(jnp.float32)
        return total.astype(jnp.bfloat16)

    def add_core(d, fx, fy, h):
        by_core[d, fx, fy, h].wait_recv()
        row, column = place(d, fx, fy, 0)
        first = pl.multiple_of(column + h * half, 128)
        mine = p_ref[pl.ds(row, rows), pl.ds(first, half)]
        sums[d, fx, fy, :, halves[h]] = wide(sums[d, fx, fy, :, halves[h]], mine)

    def first_hop_far(d):
        add_core(d, 1, 1, 0)
        by_x[d, 1] = links.send(sums.at[d, 1, 1, :, halves[0]], from_x.at[d, 1], fx=1)
        add_core(d, 1, 1, 1)
        by_y[d, 1] = links.send(sums.at[d, 1, 1, :, halves[1]], from_y.at[d, 1], fy=1)
        add_core(d, 1, 0, 0)
        by_x[d, 0] = links.send(sums.at[d, 1, 0, :, halves[0]], from_x.at[d, 0], fx=1)
        add_core(d, 1, 0, 1)

    def first_hop_near(d):
        add_core(d, 0, 1, 1)
        by_y[d, 0] = links.send(sums.at[d, 0, 1, :, halves[1]], from_y.at[d, 0], fy=1)
        add_core(d, 0, 1, 0)
        add_core(d, 0, 0, 0)
        add_core(d, 0, 0, 1)

    def second_hop(d):
        by_x[d, 1].wait_recv()
        sums[d, 0, 1, :, halves[0]] = wide(sums[d, 0, 1, :, halves[0]], from_x[d, 1])
        by_y2[d] = links.send(sums.at[d, 0, 1, :, halves[0]], second_y.at[d], fy=1)
        by_y[d, 1].wait_recv()
        sums[d, 1, 0, :, halves[1]] = wide(sums[d, 1, 0, :, halves[1]], from_y[d, 1])
        by_x2[d] = links.send(sums.at[d, 1, 0, :, halves[1]], second_x.at[d], fx=1)

    def third_hop(d):
        by_x[d, 0].wait_recv()
        by_y2[d].wait_recv()
        sums[d, 0, 0, :, halves[0]] = wide(
            sums[d, 0, 0, :, halves[0]], from_x[d, 0], second_y[d]
        )
        by_y[d, 0].wait_recv()
        by_x2[d].wait_recv()
        sums[d, 0, 0, :, halves[1]] = wide(
            sums[d, 0, 0, :, halves[1]], from_y[d, 0], second_x[d]
        )
        if d:
            by_z[d] = links.send(sums.at[d, 0, 0], from_z.at[d - 1], dz=d)

    parts = ((1, 0), (1, 1), (0, 1), (0, 0))

    def part_start(fx, h):
        return pl.multiple_of(links.flip(links.x, fx) * width + h * half, 256)

    loads = {}
    for i, part in enumerate(parts):
        columns = pl.ds(part_start(*part), half)
        loads[part] = pltpu.make_async_copy(
            down_ref.at[0, :, columns], down_held.at[:, columns], local_sem.at[i]
        )
        loads[part].start()
    shares = shares_ref[...]
    lanes = lax.broadcasted_iota(jnp.int32, shares.shape, 1)
    share = jnp.sum(
        jnp.where(lanes == lax.axis_index("expert"), shares, 0.0), axis=1, keepdims=True
    )

    def produce(fx, h):
        loads[fx, h].wait()
        first = part_start(fx, h)

        @pl.loop(0, half // 256)
        def _(tile):
            columns = pl.ds(pl.multiple_of(first + tile * 256, 256), 256)
            product = jnp.dot(
                hidden_ref[...], down_held[:, columns], preferred_element_type=jnp.float32
            )
            p_ref[:, columns] = (product * share).astype(p_ref.dtype)

        for d in order:
            for fy in (1, 0):
                row, _ = place(d, fx, fy, 1)
                by_core[d, fx, fy, h] = links.send(
                    p_ref.at[pl.ds(row, rows), pl.ds(first, half)],
                    sums.at[d, fx, fy, :, halves[h]],
                    fc=1,
                )

    links.greet()
    for part in parts[:3]:
        produce(*part)
    for d in order[:2]:
        first_hop_far(d)
    produce(*parts[3])
    for step in range(6):
        if 2 <= step < 4:
            first_hop_far(order[step])
        if step < 4:
            first_hop_near(order[step])
        if 0 <= step - 1 < 4:
            second_hop(order[step - 1])
        if step >= 2:
            third_hop(order[step - 2])
    for d in (1, 3, 2):
        by_z[d].wait_recv()
    for h in range(2):
        out_ref[:, halves[h]] = wide(
            sums[0, 0, 0, :, halves[h]],
            from_z[0, :, halves[h]],
            from_z[1, :, halves[h]],
            from_z[2, :, halves[h]],
        )
    links.finish()


def scatter_rows(hidden, shares, w_down):
    count, full = hidden.shape[0], w_down.shape[2]
    rows, width = count // lax.axis_size("expert"), full // lax.axis_size("attn")
    kind = hidden.dtype
    return pl.pallas_call(
        scatter_kernel,
        out_shape=jax.ShapeDtypeStruct((rows, width), kind),
        in_specs=[
            pl.BlockSpec(memory_space=pltpu.VMEM),
            pl.BlockSpec(memory_space=pltpu.VMEM),
            pl.BlockSpec(memory_space=pl.ANY),
        ],
        out_specs=pl.BlockSpec(memory_space=pltpu.VMEM),
        scratch_shapes=[
            pltpu.VMEM((count, full), kind),
            pltpu.VMEM(w_down.shape[1:], kind),
            pltpu.VMEM((4, 2, 2, rows, width), kind),
            pltpu.VMEM((4, 2, rows, width // 2), kind),
            pltpu.VMEM((4, 2, rows, width // 2), kind),
            pltpu.VMEM((4, rows, width // 2), kind),
            pltpu.VMEM((4, rows, width // 2), kind),
            pltpu.VMEM((3, rows, width), kind),
            pltpu.SemaphoreType.DMA((scatter_copies,)),
            pltpu.SemaphoreType.DMA((scatter_copies,)),
            pltpu.SemaphoreType.DMA((4,)),
        ],
        compiler_params=pltpu.CompilerParams(
            collective_id=1, has_side_effects=True, vmem_limit_bytes=48 * 1024 * 1024
        ),
    )(hidden, shares, w_down)


def local(
    queries,
    prompt_cache,
    beam_cache,
    new_latent,
    parents,
    lengths,
    up_values,
    moe_input,
    routes,
    route_scores,
    w_gate,
    w_up,
    w_down,
):
    row_count, head_count, key_width = queries.shape
    prompt_count = prompt_cache.shape[0]
    beam_count = row_count // prompt_count
    latent_width = up_values.shape[1]
    parent_rows = jnp.arange(row_count) // beam_count * beam_count + parents
    picked = jnp.take(beam_cache, parent_rows, axis=0)
    attend = partial(attend_prompt, latent_width=latent_width)
    latents = jax.vmap(attend)(
        queries.reshape(prompt_count, beam_count, head_count, key_width),
        prompt_cache,
        picked.reshape(prompt_count, beam_count, -1, key_width),
        new_latent.reshape(prompt_count, beam_count, key_width),
        lengths,
    )
    latents = latents.reshape(row_count, head_count, latent_width)
    attn_values = (
        jnp.einsum("rhl,hlv->rhv", latents, up_values, preferred_element_type=jnp.float32)
        .astype(jnp.bfloat16)
        .reshape(row_count, -1)
    )
    experts = lax.axis_size("expert")
    if experts == 16 and lax.axis_size("attn") == 2:
        hidden, shares = gather_rows(moe_input, routes, route_scores, w_gate, w_up)
        moe_out = scatter_rows(hidden, shares, w_down)
    else:
        own_shares = expert_shares(routes, route_scores, experts)
        shares = lax.all_gather(own_shares, "expert", axis=0, tiled=True)
        rows = lax.all_gather(moe_input, "expert", axis=0, tiled=True)
        rows = lax.all_gather(rows, "attn", axis=1, tiled=True)
        row_share = lax.dynamic_index_in_dim(
            shares, lax.axis_index("expert"), axis=1, keepdims=False
        )
        scaled = expert_block(rows, row_share, w_gate, w_up, w_down)
        halves = lax.psum_scatter(scaled, "attn", scatter_dimension=1, tiled=True)
        moe_out = lax.psum_scatter(halves, "expert", scatter_dimension=0, tiled=True)
    return (attn_values, moe_out)


def solution(mesh):
    in_specs = (
        P("expert", "attn", None),
        P("expert", None, None),
        P("expert", None, None),
        P("expert", None),
        P("expert"),
        P("expert"),
        P("attn", None, None),
        P("expert", "attn"),
        P("expert", None),
        P("expert", None),
        P("expert", None, "attn"),
        P("expert", None, "attn"),
        P("expert", "attn", None),
    )
    out_specs = (P("expert", "attn"), P("expert", "attn"))
    return jax.shard_map(local, mesh=mesh, in_specs=in_specs, out_specs=out_specs, check_vma=False)
```
